32 devices in a mesh: pipe: 2 (over core), tensor: 4 (over z), dp: 4 (over y, x).
Axes of the slice: x: 2, y: 2, z: 4, core: 2. Of those that a mesh axis runs over, the one named last changes fastest.
Arguments:
- features: float32 [16, 448, 768], P('dp', 'tensor'), may hold values from -6 to 6
- cotangent: float32 [16, 448, 768], P('dp', 'tensor'), may hold values from -6 to 6
- norm_gains: float32 [2, 2, 768], P('pipe'), may hold values from 0.1 to 1.9
- norm_shifts: float32 [2, 2, 768], P('pipe'), may hold values from -1.75 to 1.75
- qkv_weight: bfloat16 [2, 768, 12, 192], P('pipe', None, 'tensor'), may hold values from -0.21875 to 0.21875
- qv_bias: float32 [2, 2, 12, 64], P('pipe', None, 'tensor'), may hold values from -1.75 to 1.75
- out_weight: bfloat16 [2, 12, 64, 768], P('pipe', 'tensor'), may hold values from -1.25 to 1.25
- out_bias: float32 [2, 2, 768], P('pipe'), may hold values from -1.75 to 1.75
- up_weight: bfloat16 [2, 768, 3072], P('pipe', None, 'tensor'), may hold values from -0.21875 to 0.21875
- up_bias: float32 [2, 3072], P('pipe', 'tensor'), may hold values from -1.75 to 1.75
- down_weight: bfloat16 [2, 3072, 768], P('pipe', 'tensor'), may hold values from -0.109375 to 0.109375
Outputs:
- boundary: float32 [2, 16, 448, 768], P('pipe', 'dp', 'tensor')
- gain_grads: float32 [2, 2, 768], P('pipe')
- shift_grads: float32 [2, 2, 768], P('pipe')
- qkv_grads: float32 [2, 768, 12, 192], P('pipe', None, 'tensor')
- qv_bias_grads: float32 [2, 2, 12, 64], P('pipe', None, 'tensor')
- out_grads: float32 [2, 12, 64, 768], P('pipe', 'tensor')
- out_bias_grads: float32 [2, 2, 768], P('pipe')
- up_grads: float32 [2, 768, 3072], P('pipe', None, 'tensor')
- up_bias_grads: float32 [2, 3072], P('pipe', 'tensor')
- down_grads: float32 [2, 3072, 768], P('pipe', 'tensor')
The draws below stay inside these ranges and needn't reach their ends.
All inputs are finite; a program needn't handle non-finite values.
Results may differ from the reference program's by a relative error of at most 0.018.
Values may be sent and summed in bfloat16 or wider, within the bound.
A program may use at most 192 MiB of HBM per device.

```python
import jax
import jax.numpy as jnp
from jax import lax

D = 768
HEADS = 12
HDIM = 64
FF = 3072
SEQ = 448
CLIPS = 16


def block_levels(own_key, extent, shards, smallest, high):
    def one(axis_at, parts):
        heights = jax.random.uniform(jax.random.fold_in(jax.random.fold_in(own_key, 6), axis_at), (parts,), jnp.float32, smallest / len(shards), high / len(shards))
        return jnp.repeat(jnp.exp(heights), extent[axis_at] // parts).reshape((-1,) + (1,) * (len(extent) - axis_at - 1))

    factor_of = one(*shards[0])
    for cut in shards[1:]:
        factor_of = factor_of * one(*cut)
    return factor_of


def bell_draw(stream_key, shape, scale, most, cuts=(), kind=jnp.bfloat16):
    entries = jax.random.normal(stream_key, shape, jnp.float32) * scale
    if len(cuts) > 0:
        entries = block_levels(stream_key, shape, cuts, -0.22, 0.18) * entries
    return jnp.clip(entries, min=-most, max=most).astype(kind)


def setup_inputs(seed: int = 0) -> dict:
    splits = jax.random.split(jax.random.key(seed), 12)
    return {
        "features": bell_draw(splits[0], (CLIPS, SEQ, D), 1.0, 6.0, ((0, 4), (1, 4)), jnp.float32),
        "cotangent": bell_draw(splits[1], (CLIPS, SEQ, D), 1.0, 6.0, ((0, 4), (1, 4)), jnp.float32),
        "norm_gains": jnp.clip(1.0 + 0.18 * jax.random.normal(splits[2], (2, 2, D), jnp.float32), 0.1, 1.9),
        "norm_shifts": bell_draw(splits[3], (2, 2, D), 0.3, 1.75, ((0, 2),), jnp.float32),
        "qkv_weight": bell_draw(splits[4], (2, D, HEADS, 3 * HDIM), D ** -0.5, 0.21875, ((0, 2), (2, 4))),
        "qv_bias": bell_draw(splits[5], (2, 2, HEADS, HDIM), 0.3, 1.75, ((0, 2), (2, 4)), jnp.float32),
        "out_weight": bell_draw(splits[6], (2, HEADS, HDIM, D), (HEADS * HDIM // 32) ** -0.5, 1.25, ((0, 2), (1, 4))),
        "out_bias": bell_draw(splits[7], (2, 2, D), 0.3, 1.75, ((0, 2),), jnp.float32),
        "up_weight": bell_draw(splits[8], (2, D, FF), D ** -0.5, 0.21875, ((0, 2), (2, 4))),
        "up_bias": bell_draw(splits[9], (2, FF), 0.3, 1.75, ((0, 2), (1, 4)), jnp.float32),
        "down_weight": bell_draw(splits[10], (2, FF, D), FF ** -0.5, 0.109375, ((0, 2), (1, 4))),
    }


EPSILON = 1e-05
PRECISE = lax.Precision.HIGHEST

@jax.custom_vjp
def low(v):
    return lax.optimization_barrier(v.astype(jnp.bfloat16)).astype(jnp.float32)

@jax.custom_vjp
def low_back(v):
    return v

def low_keep(v):
    return (low(v), None)

def low_pass(kept, grad):
    return (grad,)

def back_keep(v):
    return (v, None)

def back_low(kept, grad):
    return (low(grad),)
low.defvjp(low_keep, low_pass)
low_back.defvjp(back_keep, back_low)

def norm_rows(values, gain_row, shift_row):
    row_mean = lax.optimization_barrier(jnp.mean(values, axis=-1, keepdims=True))
    centered = values - row_mean
    variance = lax.optimization_barrier(jnp.mean(centered * centered, axis=-1, keepdims=True))
    return centered * lax.rsqrt(variance + EPSILON) * gain_row + shift_row

def softmax_rows(scores):
    row_peak = lax.optimization_barrier(jnp.max(scores, axis=-1, keepdims=True))
    powers = jnp.exp(scores - row_peak)
    return powers / lax.optimization_barrier(jnp.sum(powers, axis=-1, keepdims=True))

def encoder_layer(params, clip_rows):
    norm_gain, norm_shift, qkv_weight, qv_bias, out_weight, out_bias, up_weight, up_bias, down_weight = params
    score_scale = HDIM ** (-0.5)
    normed = low(norm_rows(clip_rows, norm_gain[0], norm_shift[0]))
    projected = jnp.einsum('td,dhe->the', normed, qkv_weight, precision=PRECISE)
    queries = low(low_back(projected[:, :, :HDIM] + qv_bias[0]))
    key_rows = low(low_back(projected[:, :, HDIM:2 * HDIM]))
    values = low(low_back(projected[:, :, 2 * HDIM:] + qv_bias[1]))
    scores = low_back(jnp.einsum('qhe,khe->hqk', queries, key_rows, precision=PRECISE) * score_scale)
    probability = low(softmax_rows(scores))
    attended = low(low_back(jnp.einsum('hqk,khe->qhe', probability, values, precision=PRECISE)))
    branch = low_back(jnp.einsum('qhe,hed->qd', attended, out_weight, precision=PRECISE))
    middle = clip_rows + branch + out_bias[0]
    normed_two = low(norm_rows(middle, norm_gain[1], norm_shift[1]))
    hidden_pre = low_back(jnp.dot(normed_two, up_weight, precision=PRECISE) + up_bias)
    active = low(jax.nn.gelu(hidden_pre, approximate=False))
    mixed = low_back(jnp.dot(active, down_weight, precision=PRECISE))
    return middle + mixed + out_bias[1]

def reference(features, cotangent, norm_gains, norm_shifts, qkv_weight, qv_bias, out_weight, out_bias, up_weight, up_bias, down_weight):
    params = tuple((element.astype(jnp.float32) for element in (norm_gains, norm_shifts, qkv_weight, qv_bias, out_weight, out_bias, up_weight, up_bias, down_weight)))

    def stacked_pair(weights, clip_rows):
        first_layer = tuple((element[0] for element in weights))
        second_layer = tuple((element[1] for element in weights))
        return encoder_layer(second_layer, encoder_layer(first_layer, clip_rows))

    def one_clip(totals, pair_rows):
        clip_rows, seed_grad = pair_rows
        result, pullback = jax.vjp(stacked_pair, params, clip_rows.astype(jnp.float32))
        weight_grads, rows_grad = pullback(seed_grad.astype(jnp.float32))
        totals = tuple((running + gradient for running, gradient in zip(totals, weight_grads)))
        return (totals, (rows_grad, result))
    initial = tuple((jnp.zeros(element.shape, jnp.float32) for element in params))
    totals, (input_grads, outputs) = lax.scan(one_clip, initial, (features, cotangent))
    boundary = jnp.stack([input_grads, outputs])
    return (boundary, totals[0], totals[1], totals[2], totals[3], totals[4], totals[5], totals[6], totals[7], totals[8])
```

```python
import functools

import jax
import jax.numpy as jnp
from jax import lax
from jax.experimental import pallas as pl
from jax.experimental.pallas import tpu as pltpu
from jax.sharding import PartitionSpec as P

EPSILON = 1e-05
MESH = pl.DeviceIdType.MESH
f32 = jnp.float32
bf16 = jnp.bfloat16


def swap_pipe(block):
    return lax.ppermute(block, "pipe", [(0, 1), (1, 0)])


def norm_stats(values):
    row_mean = jnp.mean(values, axis=-1, keepdims=True)
    centered = values - row_mean
    variance = jnp.mean(centered * centered, axis=-1, keepdims=True)
    scale = lax.rsqrt(variance + EPSILON)
    return centered * scale, scale


def norm_back(normed_grad, values, gain_row):
    normed, scale = norm_stats(values)
    scaled = normed_grad * gain_row
    return scale * (
        scaled
        - jnp.mean(scaled, axis=-1, keepdims=True)
        - normed * jnp.mean(scaled * normed, axis=-1, keepdims=True)
    )


def exact_gelu(values):
    return jax.nn.gelu(values, approximate=False)


def greet(peers):
    barrier = pltpu.get_barrier_semaphore()
    for peer in peers:
        pl.semaphore_signal(barrier, inc=1, device_id={"tensor": peer}, device_id_type=MESH)
    pl.semaphore_wait(barrier, len(peers))


def remote(src, dst, send_sem, recv_sem, peer):
    return pltpu.make_async_remote_copy(
        src_ref=src,
        dst_ref=dst,
        send_sem=send_sem,
        recv_sem=recv_sem,
        device_id={"tensor": peer},
        device_id_type=MESH,
    )


def peers_of(group):
    me = lax.axis_index("tensor")
    return me, [lax.rem(me + k, group) for k in range(1, group)]


def gather_kernel(group, value_ref, gain_ref, shift_ref, full_ref, own, send_sem, recv_sem):
    me, peers = peers_of(group)
    greet(peers)
    copies = []
    for c in range(value_ref.shape[0]):
        normed, _ = norm_stats(value_ref[c])
        own[c] = (normed * gain_ref[...] + shift_ref[...]).astype(bf16)
        for k, peer in enumerate(peers):
            copy = remote(
                own.at[c], full_ref.at[c, me], send_sem.at[c, k], recv_sem.at[c, k], peer
            )
            copy.start()
            copies.append(copy)
        full_ref[c, me] = own[c]
    for copy in copies:
        copy.wait()


def exchange_kernel(group, transpose, mode, *refs):
    if mode == "forward":
        act, weight, resid, bias, gain, shift, value_out, full_out, *scratch = refs
    elif mode == "backward":
        act, weight, resid, saved, gain, sum_out, value_out, full_out, *scratch = refs
    else:
        act, weight, sum_out, *scratch = refs
    if mode == "sum":
        pieces, landed, send_sem, recv_sem = scratch
    else:
        pieces, landed, own, send_sem, recv_sem, send_two, recv_two = scratch
    me, peers = peers_of(group)
    clips = act.shape[0]
    contract = (((1,), (1,)), ((), ())) if transpose else (((1,), (0,)), ((), ()))

    def product(c, j):
        return lax.dot_general(act[c, j], weight[...], contract, preferred_element_type=f32)

    greet(peers)
    copies = {}
    for c in range(clips):
        for k, peer in enumerate(peers):
            pieces[c, k] = product(c, peer).astype(bf16)
            copies[c, k] = remote(
                pieces.at[c, k], landed.at[c, k], send_sem.at[c, k], recv_sem.at[c, k], peer
            )
            copies[c, k].start()
    waits = []
    for c in range(clips):
        total = product(c, me)
        for k in range(group - 1):
            copies[c, k].wait()
            total = total + landed[c, k].astype(f32)
        if mode == "sum":
            sum_out[c] = total
            continue
        if mode == "forward":
            value = resid[c] + total + bias[...]
            value_out[c] = value
            normed, _ = norm_stats(value)
            own[c] = (normed * gain[...] + shift[...]).astype(bf16)
        else:
            sum_out[c] = total
            value = resid[c] + norm_back(total, saved[c], gain[...])
            value_out[c] = value
            own[c] = value.astype(bf16)
        for k, peer in enumerate(peers):
            copy = remote(
                own.at[c], full_out.at[c, me], send_two.at[c, k], recv_two.at[c, k], peer
            )
            copy.start()
            waits.append(copy)
        full_out[c, me] = own[c]
    for copy in waits:
        copy.wait()


VMEM = pl.BlockSpec(memory_space=pltpu.VMEM)
DMA = pltpu.SemaphoreType.DMA


def params(number):
    return pltpu.CompilerParams(
        collective_id=number, has_side_effects=True, vmem_limit_bytes=40 * 1024 * 1024
    )


def gather_normed(rows, gain, shift):
    group = lax.axis_size("tensor")
    clips, share, width = rows.shape
    full = pl.pallas_call(
        functools.partial(gather_kernel, group),
        out_shape=jax.ShapeDtypeStruct((clips, group, share, width), bf16),
        in_specs=[VMEM] * 3,
        out_specs=VMEM,
        scratch_shapes=[
            pltpu.VMEM((clips, share, width), bf16),
            DMA((clips, group - 1)),
            DMA((clips, group - 1)),
        ],
        compiler_params=params(0),
        name="gather_normed",
    )(rows, gain[None], shift[None])
    return full.reshape(clips * group * share, width)


def exchange(mode, number, act, weight, transpose, share, *rest):
    group = lax.axis_size("tensor")
    width = weight.shape[0] if transpose else weight.shape[1]
    depth = act.shape[-1]
    act = act.reshape(-1, group, share, depth)
    clips = act.shape[0]
    rows = jax.ShapeDtypeStruct((clips, share, width), f32)
    full = jax.ShapeDtypeStruct((clips, group, share, width), bf16)
    outs = {"forward": (rows, full), "backward": (rows, rows, full), "sum": (rows,)}[mode]
    sems = [DMA((clips, group - 1)), DMA((clips, group - 1))]
    block = pltpu.VMEM((clips, group - 1, share, width), bf16)
    scratch = [block, block]
    if mode != "sum":
        scratch = scratch + [pltpu.VMEM((clips, share, width), bf16)] + sems
    scratch = scratch + sems
    rest = tuple(item[None] if item.ndim == 1 else item for item in rest)
    got = pl.pallas_call(
        functools.partial(exchange_kernel, group, transpose, mode),
        out_shape=outs,
        in_specs=[VMEM] * (2 + len(rest)),
        out_specs=tuple(VMEM for _ in outs),
        scratch_shapes=scratch,
        compiler_params=params(number),
        name=mode + "_exchange",
    )(act, weight, *rest)
    if mode == "sum":
        return got[0]
    return got[:-1] + (got[-1].reshape(clips * group * share, width),)


def shifted(block, distance):
    size = lax.axis_size("tensor")
    return lax.ppermute(block, "tensor", [(i, (i + distance) % size) for i in range(size)])


def gather_rows(block):
    size = lax.axis_size("tensor")
    me = lax.axis_index("tensor")
    clips, share, width = block.shape
    full = jnp.zeros((clips, size, share, width), block.dtype)
    for k in range(size):
        part = block if k == 0 else shifted(block, k)
        full = lax.dynamic_update_slice(full, part[:, None], (0, (me - k) % size, 0, 0))
    return full.reshape(clips * size * share, width)


def sum_rows(pieces):
    size = lax.axis_size("tensor")
    me = lax.axis_index("tensor")
    total = None
    for k in range(size):
        part = lax.dynamic_index_in_dim(pieces, (me + k) % size, 1, keepdims=False)
        part = part if k == 0 else shifted(part, k)
        total = part.astype(f32) if total is None else total + part.astype(f32)
    return total


def per_device(
    features,
    cotangent,
    norm_gains,
    norm_shifts,
    qkv_weight,
    qv_bias,
    out_weight,
    out_bias,
    up_weight,
    up_bias,
    down_weight,
):
    section = lax.axis_index("pipe")
    leading = section == 0
    share, width = features.shape[1:]
    group = lax.axis_size("tensor")
    length = share * group
    heads = qkv_weight.shape[2]
    hdim = qv_bias.shape[3]
    hidden = up_weight.shape[2]
    scale = hdim ** (-0.5)
    half = features.shape[0] // 2

    def both(block):
        other = swap_pipe(block)
        return jnp.where(leading, block, other), jnp.where(leading, other, block)

    qkv = both(qkv_weight[0].reshape(width, heads * 3 * hdim))
    out = both(out_weight[0].reshape(heads * hdim, width))
    up = both(up_weight[0])
    down = both(down_weight[0])
    small = [norm_gains, norm_shifts, qv_bias, out_bias, up_bias]
    packed = jnp.concatenate([item.reshape(-1) for item in small])
    unpacked = []
    for vector in both(packed):
        at, parts = 0, []
        for item in small:
            parts.append(vector[at : at + item.size].reshape(item.shape[1:]))
            at += item.size
        unpacked.append(parts)

    rows = lax.dynamic_slice_in_dim(features, section * half, half, 0)
    top_grad = lax.dynamic_slice_in_dim(cotangent, section * half, half, 0)
    grads_full = gather_rows(top_grad.astype(bf16))

    entries, middles, gathered, gathered_two, attn, mlp = [], [], [], [], [], []
    full = gather_normed(rows, unpacked[0][0][0], unpacked[0][1][0])
    for l in range(2):
        gain, shift, qv, ends, up_vector = unpacked[l]
        entries.append(rows)
        gathered.append(full)
        projected = jnp.dot(full, qkv[l], preferred_element_type=f32)
        projected = projected.reshape(half, length, heads, 3 * hdim)
        queries = (projected[..., :hdim] + qv[0]).astype(bf16)
        keys = projected[..., hdim : 2 * hdim].astype(bf16)
        values = (projected[..., 2 * hdim :] + qv[1]).astype(bf16)
        scores = jnp.einsum("bqhe,bkhe->bhqk", queries, keys, preferred_element_type=f32) * scale
        powers = jnp.exp(scores - jnp.max(scores, axis=-1, keepdims=True))
        prob = powers / jnp.sum(powers, axis=-1, keepdims=True)
        prob_low = prob.astype(bf16)
        attended = jnp.einsum("bhqk,bkhe->bqhe", prob_low, values, preferred_element_type=f32)
        attended = attended.astype(bf16).reshape(half * length, heads * hdim)
        attn.append((queries, keys, values, prob, prob_low, attended))
        middle, full = exchange(
            "forward", 1, attended, out[l], False, share, rows, ends[0], gain[1], shift[1]
        )
        middles.append(middle)
        gathered_two.append(full)
        pre = jnp.dot(full, up[l], preferred_element_type=f32) + up_vector
        active = exact_gelu(pre).astype(bf16)
        mlp.append((pre, active))
        if l == 0:
            rows, full = exchange(
                "forward", 2, active, down[l], False, share, middle, ends[1],
                unpacked[1][0][0], unpacked[1][1][0],
            )
        else:
            pieces = jnp.dot(active, down[l], preferred_element_type=f32).astype(bf16)
            pieces = pieces.reshape(half, group, share, width)
            result = middle + sum_rows(pieces) + ends[1]

    layer_grads = [None, None]
    shared = [None, None]
    incoming = top_grad
    for l in (1, 0):
        gain, shift, qv, ends, up_vector = unpacked[l]
        pre, active = mlp[l]
        down_grad = jnp.einsum("nf,nd->fd", active, grads_full, preferred_element_type=f32)
        active_grad = jnp.einsum("nd,fd->nf", grads_full, down[l], preferred_element_type=f32)
        pre_grad = jax.vjp(exact_gelu, pre)[1](active_grad)[0].astype(bf16)
        up_bias_grad = jnp.sum(pre_grad.astype(f32), axis=0)
        up_grad = jnp.einsum("nd,nf->df", gathered_two[l], pre_grad, preferred_element_type=f32)
        sum_two, middle_grad, full = exchange(
            "backward", 3, pre_grad, up[l], True, share, incoming, middles[l], gain[1]
        )
        normed_two = norm_stats(middles[l])[0]
        queries, keys, values, prob, prob_low, attended = attn[l]
        out_grad = jnp.einsum("nc,nd->cd", attended, full, preferred_element_type=f32)
        attended_grad = jnp.einsum("nd,cd->nc", full, out[l], preferred_element_type=f32)
        attended_grad = attended_grad.astype(bf16).reshape(half, length, heads, hdim)
        prob_grad = jnp.einsum(
            "bqhe,bkhe->bhqk", attended_grad, values, preferred_element_type=f32
        )
        values_grad = jnp.einsum(
            "bhqk,bqhe->bkhe", prob_low, attended_grad, preferred_element_type=f32
        ).astype(bf16)
        inner = jnp.sum(prob * prob_grad, axis=-1, keepdims=True)
        scores_grad = (prob * (prob_grad - inner)).astype(bf16)
        queries_grad = (
            jnp.einsum("bhqk,bkhe->bqhe", scores_grad, keys, preferred_element_type=f32) * scale
        ).astype(bf16)
        keys_grad = (
            jnp.einsum("bhqk,bqhe->bkhe", scores_grad, queries, preferred_element_type=f32) * scale
        ).astype(bf16)
        flat = jnp.concatenate([queries_grad, keys_grad, values_grad], axis=-1)
        flat = flat.reshape(half * length, heads * 3 * hdim)
        bias_grad = jnp.stack(
            [
                jnp.sum(queries_grad.astype(f32), axis=(0, 1)),
                jnp.sum(values_grad.astype(f32), axis=(0, 1)),
            ]
        )
        qkv_grad = jnp.einsum("nd,nc->dc", gathered[l], flat, preferred_element_type=f32)
        end_grads = [jnp.sum(middle_grad, axis=(0, 1)), jnp.sum(incoming, axis=(0, 1))]
        if l == 1:
            sum_one, entry_grad, grads_full = exchange(
                "backward", 4, flat, qkv[l], True, share, middle_grad, entries[l], gain[0]
            )
        else:
            sum_one = exchange("sum", 5, flat, qkv[l], True, share)
            entry_grad = middle_grad + norm_back(sum_one, entries[l], gain[0])
        normed_one = norm_stats(entries[l])[0]
        shared[l] = jnp.stack(
            [
                jnp.sum(sum_one * normed_one, axis=(0, 1)),
                jnp.sum(sum_two * normed_two, axis=(0, 1)),
                jnp.sum(sum_one, axis=(0, 1)),
                jnp.sum(sum_two, axis=(0, 1)),
            ]
            + end_grads
        )
        layer_grads[l] = (
            qkv_grad,
            out_grad,
            up_grad,
            down_grad,
            jnp.concatenate([bias_grad.reshape(-1), up_bias_grad]),
        )
        incoming = entry_grad

    def reduced(first, second):
        mine = jnp.where(leading, first, second)
        other = jnp.where(leading, second, first)
        return mine + swap_pipe(other.astype(bf16)).astype(f32)

    summed = [
        lax.psum(reduced(a, b).astype(bf16), "dp").astype(f32) for a, b in zip(*layer_grads)
    ]
    common = jnp.where(leading, shared[0], shared[1]) + swap_pipe(
        jnp.where(leading, shared[1], shared[0])
    )
    common = lax.psum(common, ("tensor", "dp"))
    given = swap_pipe(jnp.where(leading, result, entry_grad))
    boundary = jnp.where(
        leading,
        jnp.concatenate([entry_grad, given]),
        jnp.concatenate([given, result]),
    )
    bias_size = 2 * heads * hdim
    return (
        boundary[None],
        common[None, 0:2],
        common[None, 2:4],
        summed[0].reshape(1, width, heads, 3 * hdim),
        summed[4][:bias_size].reshape(1, 2, heads, hdim),
        summed[1].reshape(1, heads, hdim, width),
        common[None, 4:6],
        summed[2][None],
        summed[4][bias_size:][None],
        summed[3][None],
    )


def solution(mesh):
    in_specs = (
        P("dp", "tensor", None),
        P("dp", "tensor", None),
        P("pipe", None, None),
        P("pipe", None, None),
        P("pipe", None, "tensor", None),
        P("pipe", None, "tensor", None),
        P("pipe", "tensor", None, None),
        P("pipe", None, None),
        P("pipe", None, "tensor"),
        P("pipe", "tensor"),
        P("pipe", "tensor", None),
    )
    out_specs = (
        P("pipe", "dp", "tensor", None),
        P("pipe", None, None),
        P("pipe", None, None),
        P("pipe", None, "tensor", None),
        P("pipe", None, "tensor", None),
        P("pipe", "tensor", None, None),
        P("pipe", None, None),
        P("pipe", None, "tensor"),
        P("pipe", "tensor"),
        P("pipe", "tensor", None),
    )
    return jax.shard_map(
        per_device, mesh=mesh, in_specs=in_specs, out_specs=out_specs, check_vma=False
    )
```

```python
import functools

import jax
import jax.numpy as jnp
from jax import lax
from jax.experimental import pallas as pl
from jax.experimental.pallas import tpu as pltpu
from jax.sharding import PartitionSpec as P

EPSILON = 1e-05
MESH = pl.DeviceIdType.MESH
f32 = jnp.float32
bf16 = jnp.bfloat16


def swap_pipe(block):
    return lax.ppermute(block, "pipe", [(0, 1), (1, 0)])


def norm_stats(values):
    row_mean = jnp.mean(values, axis=-1, keepdims=True)
    centered = values - row_mean
    variance = jnp.mean(centered * centered, axis=-1, keepdims=True)
    scale = lax.rsqrt(variance + EPSILON)
    return centered * scale, scale


def norm_back(normed_grad, values, gain_row):
    normed, scale = norm_stats(values)
    scaled = normed_grad * gain_row
    return scale * (
        scaled
        - jnp.mean(scaled, axis=-1, keepdims=True)
        - normed * jnp.mean(scaled * normed, axis=-1, keepdims=True)
    )


def exact_gelu(values):
    return jax.nn.gelu(values, approximate=False)


def greet(peers, clip_peers=()):
    barrier = pltpu.get_barrier_semaphore()
    for peer in peers:
        pl.semaphore_signal(barrier, inc=1, device_id={"tensor": peer}, device_id_type=MESH)
    for peer in clip_peers:
        pl.semaphore_signal(barrier, inc=1, device_id={"dp": peer}, device_id_type=MESH)
    pl.semaphore_wait(barrier, len(peers) + len(clip_peers))


def remote(src, dst, send_sem, recv_sem, peer, axis="tensor"):
    return pltpu.make_async_remote_copy(
        src_ref=src,
        dst_ref=dst,
        send_sem=send_sem,
        recv_sem=recv_sem,
        device_id={axis: peer},
        device_id_type=MESH,
    )


def peers_of(group):
    me = lax.axis_index("tensor")
    return me, [lax.rem(me + k, group) for k in range(1, group)]


def gather_kernel(group, value_ref, gain_ref, shift_ref, full_ref, own, send_sem, recv_sem):
    me, peers = peers_of(group)
    greet(peers)
    copies = []
    for c in range(value_ref.shape[0]):
        normed, _ = norm_stats(value_ref[c])
        own[c] = (normed * gain_ref[...] + shift_ref[...]).astype(bf16)
        for k, peer in enumerate(peers):
            copy = remote(
                own.at[c], full_ref.at[c, me], send_sem.at[c, k], recv_sem.at[c, k], peer
            )
            copy.start()
            copies.append(copy)
        full_ref[c, me] = own[c]
    for copy in copies:
        copy.wait()


def exchange_kernel(group, transpose, mode, side, clip_group, *refs):
    if side is not None:
        *refs, side_send, side_recv = refs
        at = {"backward": 5, "sum": 2}[mode]
        side_in, refs = refs[at], refs[:at] + refs[at + 1 :]
        at = {"backward": 8, "sum": 3}[mode]
        side_out, refs = refs[at], refs[:at] + refs[at + 1 :]
    if mode == "forward":
        act, weight, resid, bias, gain, shift, value_out, full_out, *scratch = refs
    elif mode == "backward":
        act, weight, resid, saved, gain, sum_out, value_out, full_out, *scratch = refs
    else:
        act, weight, sum_out, *scratch = refs
    if mode == "sum":
        pieces, landed, send_sem, recv_sem = scratch
    else:
        pieces, landed, own, send_sem, recv_sem, send_two, recv_two = scratch
    me, peers = peers_of(group)
    clips = act.shape[0]
    contract = (((1,), (1,)), ((), ())) if transpose else (((1,), (0,)), ((), ()))

    def product(c, j):
        return lax.dot_general(act[c, j], weight[...], contract, preferred_element_type=f32)

    here = lax.axis_index("dp")
    clip_peers = [] if side is None else [lax.rem(here + k, clip_group) for k in range(1, clip_group)]
    greet(peers, clip_peers)
    side_copies = []
    for k, peer in enumerate(clip_peers):
        source = side_in.at[peer] if side == "scatter" else side_in
        target = side_out.at[k] if side == "scatter" else side_out.at[here]
        copy = remote(source, target, side_send.at[k], side_recv.at[k], peer, "dp")
        copy.start()
        side_copies.append(copy)
    if side == "gather":
        side_out[here] = side_in[...]
    copies = {}
    for c in range(clips):
        for k, peer in enumerate(peers):
            pieces[c, k] = product(c, peer).astype(bf16)
            copies[c, k] = remote(
                pieces.at[c, k], landed.at[c, k], send_sem.at[c, k], recv_sem.at[c, k], peer
            )
            copies[c, k].start()
    waits = []
    for c in range(clips):
        total = product(c, me)
        for k in range(group - 1):
            copies[c, k].wait()
            total = total + landed[c, k].astype(f32)
        if mode == "sum":
            sum_out[c] = total
            continue
        if mode == "forward":
            value = resid[c] + total + bias[...]
            value_out[c] = value
            normed, _ = norm_stats(value)
            own[c] = (normed * gain[...] + shift[...]).astype(bf16)
        else:
            sum_out[c] = total
            value = resid[c] + norm_back(total, saved[c], gain[...])
            value_out[c] = value
            own[c] = value.astype(bf16)
        for k, peer in enumerate(peers):
            copy = remote(
                own.at[c], full_out.at[c, me], send_two.at[c, k], recv_two.at[c, k], peer
            )
            copy.start()
            waits.append(copy)
        full_out[c, me] = own[c]
    for copy in waits + side_copies:
        copy.wait()


VMEM = pl.BlockSpec(memory_space=pltpu.VMEM)
DMA = pltpu.SemaphoreType.DMA


def params(number):
    return pltpu.CompilerParams(
        collective_id=number, has_side_effects=True, vmem_limit_bytes=40 * 1024 * 1024
    )


def gather_normed(rows, gain, shift):
    group = lax.axis_size("tensor")
    clips, share, width = rows.shape
    full = pl.pallas_call(
        functools.partial(gather_kernel, group),
        out_shape=jax.ShapeDtypeStruct((clips, group, share, width), bf16),
        in_specs=[VMEM] * 3,
        out_specs=VMEM,
        scratch_shapes=[
            pltpu.VMEM((clips, share, width), bf16),
            DMA((clips, group - 1)),
            DMA((clips, group - 1)),
        ],
        compiler_params=params(0),
        name="gather_normed",
    )(rows, gain[None], shift[None])
    return full.reshape(clips * group * share, width)


def exchange(mode, number, act, weight, transpose, share, *rest, side=None, parcel=None):
    group = lax.axis_size("tensor")
    width = weight.shape[0] if transpose else weight.shape[1]
    depth = act.shape[-1]
    act = act.reshape(-1, group, share, depth)
    clips = act.shape[0]
    rows = jax.ShapeDtypeStruct((clips, share, width), f32)
    full = jax.ShapeDtypeStruct((clips, group, share, width), bf16)
    outs = {"forward": (rows, full), "backward": (rows, rows, full), "sum": (rows,)}[mode]
    sems = [DMA((clips, group - 1)), DMA((clips, group - 1))]
    block = pltpu.VMEM((clips, group - 1, share, width), bf16)
    scratch = [block, block]
    if mode != "sum":
        scratch = scratch + [pltpu.VMEM((clips, share, width), bf16)] + sems
    scratch = scratch + sems
    rest = tuple(item[None] if item.ndim == 1 else item for item in rest)
    clip_group = lax.axis_size("dp")
    if side is not None:
        rest = rest + (parcel,)
        count = clip_group - 1 if side == "scatter" else clip_group
        outs = outs + (jax.ShapeDtypeStruct((count,) + parcel.shape[-2:], bf16),)
        scratch = scratch + [DMA((clip_group - 1,)), DMA((clip_group - 1,))]
    got = pl.pallas_call(
        functools.partial(exchange_kernel, group, transpose, mode, side, clip_group),
        out_shape=outs,
        in_specs=[VMEM] * (2 + len(rest)),
        out_specs=tuple(VMEM for _ in outs),
        scratch_shapes=scratch,
        compiler_params=params(number),
        name=mode + "_exchange",
    )(act, weight, *rest)
    if mode == "sum":
        return got
    at = len(outs) - 1 if side is None else len(outs) - 2
    return got[:at] + (got[at].reshape(clips * group * share, width),) + got[at + 1 :]


def pack_half(grads, upper):
    parts = []
    for grad in grads:
        rows = grad.shape[0] // 2
        parts.append(lax.dynamic_slice_in_dim(grad, upper * rows, rows, 0))
    return jnp.concatenate(parts)


def shifted(block, distance):
    size = lax.axis_size("tensor")
    return lax.ppermute(block, "tensor", [(i, (i + distance) % size) for i in range(size)])


def gather_rows(block):
    size = lax.axis_size("tensor")
    me = lax.axis_index("tensor")
    clips, share, width = block.shape
    full = jnp.zeros((clips, size, share, width), block.dtype)
    for k in range(size):
        part = block if k == 0 else shifted(block, k)
        full = lax.dynamic_update_slice(full, part[:, None], (0, (me - k) % size, 0, 0))
    return full.reshape(clips * size * share, width)


def sum_rows(pieces):
    size = lax.axis_size("tensor")
    me = lax.axis_index("tensor")
    total = None
    for k in range(size):
        part = lax.dynamic_index_in_dim(pieces, (me + k) % size, 1, keepdims=False)
        part = part if k == 0 else shifted(part, k)
        total = part.astype(f32) if total is None else total + part.astype(f32)
    return total


def per_device(
    features,
    cotangent,
    norm_gains,
    norm_shifts,
    qkv_weight,
    qv_bias,
    out_weight,
    out_bias,
    up_weight,
    up_bias,
    down_weight,
):
    section = lax.axis_index("pipe")
    leading = section == 0
    share, width = features.shape[1:]
    group = lax.axis_size("tensor")
    length = share * group
    heads = qkv_weight.shape[2]
    hdim = qv_bias.shape[3]
    hidden = up_weight.shape[2]
    scale = hdim ** (-0.5)
    half = features.shape[0] // 2

    def both(block):
        other = swap_pipe(block)
        return jnp.where(leading, block, other), jnp.where(leading, other, block)

    qkv = both(qkv_weight[0].reshape(width, heads * 3 * hdim))
    out = both(out_weight[0].reshape(heads * hdim, width))
    up = both(up_weight[0])
    down = both(down_weight[0])
    small = [norm_gains, norm_shifts, qv_bias, out_bias, up_bias]
    packed = jnp.concatenate([item.reshape(-1) for item in small])
    unpacked = []
    for vector in both(packed):
        at, parts = 0, []
        for item in small:
            parts.append(vector[at : at + item.size].reshape(item.shape[1:]))
            at += item.size
        unpacked.append(parts)

    rows = lax.dynamic_slice_in_dim(features, section * half, half, 0)
    top_grad = lax.dynamic_slice_in_dim(cotangent, section * half, half, 0)
    grads_full = gather_rows(top_grad.astype(bf16))

    entries, middles, gathered, gathered_two, attn, mlp = [], [], [], [], [], []
    full = gather_normed(rows, unpacked[0][0][0], unpacked[0][1][0])
    for l in range(2):
        gain, shift, qv, ends, up_vector = unpacked[l]
        entries.append(rows)
        gathered.append(full)
        projected = jnp.dot(full, qkv[l], preferred_element_type=f32)
        projected = projected.reshape(half, length, heads, 3 * hdim)
        queries = (projected[..., :hdim] + qv[0]).astype(bf16)
        keys = projected[..., hdim : 2 * hdim].astype(bf16)
        values = (projected[..., 2 * hdim :] + qv[1]).astype(bf16)
        scores = jnp.einsum("bqhe,bkhe->bhqk", queries, keys, preferred_element_type=f32) * scale
        powers = jnp.exp(scores - jnp.max(scores, axis=-1, keepdims=True))
        prob = powers / jnp.sum(powers, axis=-1, keepdims=True)
        prob_low = prob.astype(bf16)
        attended = jnp.einsum("bhqk,bkhe->bqhe", prob_low, values, preferred_element_type=f32)
        attended = attended.astype(bf16).reshape(half * length, heads * hdim)
        attn.append((queries, keys, values, prob, prob_low, attended))
        middle, full = exchange(
            "forward", 1, attended, out[l], False, share, rows, ends[0], gain[1], shift[1]
        )
        middles.append(middle)
        gathered_two.append(full)
        pre = jnp.dot(full, up[l], preferred_element_type=f32) + up_vector
        active = exact_gelu(pre).astype(bf16)
        mlp.append((pre, active))
        if l == 0:
            rows, full = exchange(
                "forward", 2, active, down[l], False, share, middle, ends[1],
                unpacked[1][0][0], unpacked[1][1][0],
            )
        else:
            pieces = jnp.dot(active, down[l], preferred_element_type=f32).astype(bf16)
            pieces = pieces.reshape(half, group, share, width)
            result = middle + sum_rows(pieces) + ends[1]

    layer_grads = [None, None]
    shared = [None, None]
    incoming = top_grad
    for l in (1, 0):
        gain, shift, qv, ends, up_vector = unpacked[l]
        pre, active = mlp[l]
        down_grad = jnp.einsum("nf,nd->fd", active, grads_full, preferred_element_type=f32)
        active_grad = jnp.einsum("nd,fd->nf", grads_full, down[l], preferred_element_type=f32)
        pre_grad = jax.vjp(exact_gelu, pre)[1](active_grad)[0].astype(bf16)
        up_bias_grad = jnp.sum(pre_grad.astype(f32), axis=0)
        up_grad = jnp.einsum("nd,nf->df", gathered_two[l], pre_grad, preferred_element_type=f32)
        if l == 1:
            sum_two, middle_grad, full = exchange(
                "backward", 3, pre_grad, up[l], True, share, incoming, middles[l], gain[1]
            )
        else:
            sum_two, middle_grad, full, landed = exchange(
                "backward", 6, pre_grad, up[l], True, share, incoming, middles[l], gain[1],
                side="scatter", parcel=parcel,
            )
            total = lax.dynamic_index_in_dim(parcel, lax.axis_index("dp"), 0, keepdims=False)
            total = total.astype(f32) + jnp.sum(landed.astype(f32), axis=0)
            reduced_part = total.astype(bf16)
        normed_two = norm_stats(middles[l])[0]
        queries, keys, values, prob, prob_low, attended = attn[l]
        out_grad = jnp.einsum("nc,nd->cd", attended, full, preferred_element_type=f32)
        attended_grad = jnp.einsum("nd,cd->nc", full, out[l], preferred_element_type=f32)
        attended_grad = attended_grad.astype(bf16).reshape(half, length, heads, hdim)
        prob_grad = jnp.einsum(
            "bqhe,bkhe->bhqk", attended_grad, values, preferred_element_type=f32
        )
        values_grad = jnp.einsum(
            "bhqk,bqhe->bkhe", prob_low, attended_grad, preferred_element_type=f32
        ).astype(bf16)
        inner = jnp.sum(prob * prob_grad, axis=-1, keepdims=True)
        scores_grad = (prob * (prob_grad - inner)).astype(bf16)
        queries_grad = (
            jnp.einsum("bhqk,bkhe->bqhe", scores_grad, keys, preferred_element_type=f32) * scale
        ).astype(bf16)
        keys_grad = (
            jnp.einsum("bhqk,bqhe->bkhe", scores_grad, queries, preferred_element_type=f32) * scale
        ).astype(bf16)
        flat = jnp.concatenate([queries_grad, keys_grad, values_grad], axis=-1)
        flat = flat.reshape(half * length, heads * 3 * hdim)
        bias_grad = jnp.stack(
            [
                jnp.sum(queries_grad.astype(f32), axis=(0, 1)),
                jnp.sum(values_grad.astype(f32), axis=(0, 1)),
            ]
        )
        qkv_grad = jnp.einsum("nd,nc->cd", gathered[l], flat, preferred_element_type=f32)
        end_grads = [jnp.sum(middle_grad, axis=(0, 1)), jnp.sum(incoming, axis=(0, 1))]
        if l == 1:
            sum_one, entry_grad, grads_full = exchange(
                "backward", 4, flat, qkv[l], True, share, middle_grad, entries[l], gain[0]
            )
        else:
            flat, result = lax.optimization_barrier((flat, result))
            sum_one, top_half = exchange(
                "sum", 5, flat, qkv[l], True, share, side="gather", parcel=reduced_part
            )
            top_half = top_half.reshape(-1, width)
            entry_grad = middle_grad + norm_back(sum_one, entries[l], gain[0])
        normed_one = norm_stats(entries[l])[0]
        shared[l] = jnp.stack(
            [
                jnp.sum(sum_one * normed_one, axis=(0, 1)),
                jnp.sum(sum_two * normed_two, axis=(0, 1)),
                jnp.sum(sum_one, axis=(0, 1)),
                jnp.sum(sum_two, axis=(0, 1)),
            ]
            + end_grads
        )
        layer_grads[l] = jnp.concatenate([bias_grad.reshape(-1), up_bias_grad])
        grads = (qkv_grad, out_grad, up_grad, down_grad)
        given = swap_pipe(pack_half(grads, 1 - section).astype(bf16))
        half_sum = (pack_half(grads, section) + given.astype(f32)).astype(bf16)
        if l == 1:
            parcel = half_sum.reshape(lax.axis_size("dp"), -1, width)
        incoming = entry_grad

    def reduced(first, second):
        mine = jnp.where(leading, first, second)
        other = jnp.where(leading, second, first)
        return mine + swap_pipe(other.astype(bf16)).astype(f32)

    first_half = lax.psum(half_sum, "dp")
    kept = jnp.where(leading, first_half, top_half)
    other = swap_pipe(jnp.where(leading, top_half, first_half))
    lower = jnp.where(leading, kept, other)
    upper = jnp.where(leading, other, kept)
    summed, at = [], 0
    for grad in grads:
        rows = grad.shape[0] // 2
        summed.append(jnp.concatenate([lower[at : at + rows], upper[at : at + rows]]).astype(f32))
        at += rows
    vectors = lax.psum(reduced(*layer_grads), "dp")
    common = jnp.where(leading, shared[0], shared[1]) + swap_pipe(
        jnp.where(leading, shared[1], shared[0])
    )
    common = lax.psum(common, ("tensor", "dp"))
    given = swap_pipe(jnp.where(leading, result, entry_grad))
    boundary = jnp.where(
        leading,
        jnp.concatenate([entry_grad, given]),
        jnp.concatenate([given, result]),
    )
    bias_size = 2 * heads * hdim
    return (
        boundary[None],
        common[None, 0:2],
        common[None, 2:4],
        summed[0].T.reshape(1, width, heads, 3 * hdim),
        vectors[:bias_size].reshape(1, 2, heads, hdim),
        summed[1].reshape(1, heads, hdim, width),
        common[None, 4:6],
        summed[2][None],
        vectors[bias_size:][None],
        summed[3][None],
    )


def solution(mesh):
    in_specs = (
        P("dp", "tensor", None),
        P("dp", "tensor", None),
        P("pipe", None, None),
        P("pipe", None, None),
        P("pipe", None, "tensor", None),
        P("pipe", None, "tensor", None),
        P("pipe", "tensor", None, None),
        P("pipe", None, None),
        P("pipe", None, "tensor"),
        P("pipe", "tensor"),
        P("pipe", "tensor", None),
    )
    out_specs = (
        P("pipe", "dp", "tensor", None),
        P("pipe", None, None),
        P("pipe", None, None),
        P("pipe", None, "tensor", None),
        P("pipe", None, "tensor", None),
        P("pipe", "tensor", None, None),
        P("pipe", None, None),
        P("pipe", None, "tensor"),
        P("pipe", "tensor"),
        P("pipe", "tensor", None),
    )
    return jax.shard_map(
        per_device, mesh=mesh, in_specs=in_specs, out_specs=out_specs, check_vma=False
    )
```
